32 devices in a mesh: segment: 4 (over z), row: 4 (over y, x), dp: 2 (over core).
Axes of the slice: x: 2, y: 2, z: 4, core: 2. Of those that a mesh axis runs over, the one named last changes fastest.
Arguments:
- features: bfloat16 [4, 64, 64, 128], P('dp', 'row'), may hold values from -6 to 6
- residues: int32 [4], P('dp'), may hold values from 32 to 64, as said below
- blocks: int32 [4], P('segment'), may hold values from 1 to 3, as said below
- weights: bfloat16 [4, 3, 9, 128, 128], P('segment'), may hold values from -0.125 to 0.125
- cotangent: bfloat16 [4, 64, 64, 128], P('dp', 'row'), may hold values from -0.046875 to 0.046875
Outputs:
- weight_grads: float32 [4, 3, 9, 128, 128], P('segment')
The draws below stay inside these ranges and needn't reach their ends.
Inputs may be any that keep to these rules, and one draw needn't show every extreme that they name: `residues`: rows of a complex at or beyond its residue count are padding. `blocks`: slots of a section at or beyond its count are skipped.
All inputs are finite; a program needn't handle non-finite values.
Results may differ from the reference program's by a relative error of at most 0.017.
Values may be sent and summed in bfloat16 or wider, within the bound.
A program may use at most 64 MiB of HBM per device.

```python
import jax
import jax.numpy as jnp

C = 128
W = 64
SLOTS = 3
HALO = 8
SEGMENTS = 4
ROWS = 64
COMPLEXES = 4


def draw_residues(key, part):
    base = jax.random.fold_in(key, 101)
    first_key, second_key = jax.random.split(base)
    values = jax.random.randint(first_key, (COMPLEXES,), ROWS // 2, ROWS + 1)
    order = jax.random.permutation(second_key, COMPLEXES)
    values = values.at[order[0]].set(ROWS)
    values = values.at[order[1]].set(ROWS // 2)
    return values.astype(jnp.int32)


def draw_blocks(key, part):
    base = jax.random.fold_in(key, 202)
    first_key, second_key = jax.random.split(base)
    values = jax.random.randint(first_key, (SEGMENTS,), 1, SLOTS + 1)
    order = jax.random.permutation(second_key, SEGMENTS)
    values = values.at[order[0]].set(SLOTS)
    values = values.at[order[1]].set(1)
    return values.astype(jnp.int32)


def steps_of(stream_key, extent, cuts, low, largest):
    factor_of, own = 1.0, jax.random.fold_in(stream_key, 6)
    for position, shards_of in cuts:
        heights = jnp.exp(jax.random.uniform(jax.random.fold_in(own, position), (shards_of,), jnp.float32, low / len(cuts), largest / len(cuts)))
        factor_of = factor_of * jnp.repeat(heights, extent[position] // shards_of).reshape([-1 if axis == position else 1 for axis in range(len(extent))])
    return factor_of


def centred(own_key, extent, scale, most, cuts=(), held_as=jnp.bfloat16):
    array = jax.random.normal(own_key, extent, jnp.float32) * scale
    if len(cuts) > 0:
        array = steps_of(own_key, extent, cuts, -0.22, 0.18) * array
    return jnp.clip(array, min=-most, max=most).astype(held_as)


def setup_inputs(seed: int = 0) -> dict:
    seeds = jax.random.split(jax.random.key(seed), 6)
    return {
        "features": centred(seeds[0], (COMPLEXES, ROWS, W, C), 1.0, 6.0, ((0, 2), (1, 4))),
        "residues": draw_residues(jax.random.fold_in(seeds[5], 71), 0),
        "blocks": draw_blocks(jax.random.fold_in(seeds[5], 71), 0),
        "weights": centred(seeds[3], (SEGMENTS, SLOTS, 9, C, C), (18 * C) ** -0.5, 0.125, ((0, 4),)),
        "cotangent": centred(seeds[4], (COMPLEXES, ROWS, W, C), (1.0 / (COMPLEXES * ROWS * W) ** 0.5), 0.046875, ((0, 2), (1, 4))),
    }


def widen(values):
    return jnp.pad(values, ((HALO, HALO), (HALO, HALO), (0, 0)))


def elu_rounded(values):
    return jax.nn.elu(values.astype(jnp.float32)).astype(jnp.bfloat16)


def conv_taps(padded, weight_slot, dilation):
    total = jnp.zeros((ROWS * W, C), jnp.float32)
    for row_step in (-1, 0, 1):
        for col_step in (-1, 0, 1):
            tap_index = 3 * (row_step + 1) + col_step + 1
            row_start = HALO + row_step * dilation
            col_start = HALO + col_step * dilation
            piece = padded[row_start:row_start + ROWS, col_start:col_start + W]
            total = total + jnp.dot(piece.reshape(ROWS * W, C), weight_slot[tap_index], preferred_element_type=jnp.float32)
    return total.reshape(ROWS, W, C)


def backward_taps(padded_act, padded_cot, masked, weight_slot, dilation):
    flat_cot = masked.reshape(ROWS * W, C)
    terms = []
    back_sum = jnp.zeros((ROWS * W, C), jnp.float32)
    for row_step in (-1, 0, 1):
        for col_step in (-1, 0, 1):
            tap_index = 3 * (row_step + 1) + col_step + 1
            row_start = HALO + row_step * dilation
            col_start = HALO + col_step * dilation
            act_piece = padded_act[row_start:row_start + ROWS, col_start:col_start + W].reshape(ROWS * W, C)
            terms.append(jnp.dot(act_piece.T, flat_cot, preferred_element_type=jnp.float32))
            row_back = HALO - row_step * dilation
            col_back = HALO - col_step * dilation
            cot_piece = padded_cot[row_back:row_back + ROWS, col_back:col_back + W].reshape(ROWS * W, C)
            back_sum = back_sum + jnp.dot(cot_piece, weight_slot[tap_index].T, preferred_element_type=jnp.float32)
    return jnp.stack(terms), back_sum.reshape(ROWS, W, C)


def reference(features, residues, blocks, weights, cotangent):
    grads = [[jnp.zeros((9, C, C), jnp.float32) for slot_index in range(SLOTS)] for segment_index in range(SEGMENTS)]
    row_ids = jnp.arange(ROWS, dtype=jnp.int32)
    for complex_index in range(COMPLEXES):
        keep = (row_ids < residues[complex_index]).astype(jnp.float32)[:, None, None]
        resident = (features[complex_index].astype(jnp.float32) * keep).astype(jnp.bfloat16)
        stored = []
        for segment_index in range(SEGMENTS):
            for slot_index in range(SLOTS):
                dilation = 2 ** ((SLOTS * segment_index + slot_index) % 4)
                active = slot_index < blocks[segment_index]
                stored.append(resident)
                conv_sum = conv_taps(widen(elu_rounded(resident)), weights[segment_index, slot_index], dilation)
                updated = ((resident.astype(jnp.float32) + conv_sum) * keep).astype(jnp.bfloat16)
                resident = jnp.where(active, updated, resident)
        grad_now = cotangent[complex_index]
        for segment_index in reversed(range(SEGMENTS)):
            for slot_index in reversed(range(SLOTS)):
                dilation = 2 ** ((SLOTS * segment_index + slot_index) % 4)
                active = slot_index < blocks[segment_index]
                block_input = stored[segment_index * SLOTS + slot_index]
                masked = (grad_now.astype(jnp.float32) * keep).astype(jnp.bfloat16)
                terms, back_sum = backward_taps(widen(elu_rounded(block_input)), widen(masked), masked, weights[segment_index, slot_index], dilation)
                input_f = block_input.astype(jnp.float32)
                slope = jnp.where(input_f > 0, 1.0, jnp.exp(jnp.minimum(input_f, 0.0)))
                updated = (masked.astype(jnp.float32) + slope * back_sum).astype(jnp.bfloat16)
                grads[segment_index][slot_index] = grads[segment_index][slot_index] + jnp.where(active, terms, jnp.zeros_like(terms))
                grad_now = jnp.where(active, updated, grad_now)
    return jnp.stack([jnp.stack(grads[segment_index]) for segment_index in range(SEGMENTS)])
```

```python
import functools

import jax
import jax.numpy as jnp
from jax import lax
from jax.experimental import pallas as pl
from jax.experimental.pallas import tpu as pltpu
from jax.sharding import PartitionSpec as P

HALO = 8


def padded_2(block, sides, width):
    for axis, dim in sides:
        count = lax.axis_size(axis)
        forward = [(i, i + 1) for i in range(count - 1)]
        backward = [(target, source) for source, target in forward]
        low = lax.ppermute(
            lax.slice_in_dim(block, block.shape[dim] - width, None, axis=dim), axis, forward
        )
        high = lax.ppermute(lax.slice_in_dim(block, 0, width, axis=dim), axis, backward)
        block = jnp.concatenate([low, block, high], axis=dim)
    return block


def passed_along(value, axis, steps):
    count = lax.axis_size(axis)
    leading, last = (max(0, -steps), min(count, count - steps))
    return lax.ppermute(value, axis, [(source, source + steps) for source in range(leading, last)])


def widen_columns(values):
    return jnp.pad(values, ((0, 0), (HALO, HALO), (0, 0)))


def elu_rounded(values):
    return jax.nn.elu(values.astype(jnp.float32)).astype(jnp.bfloat16)


def shifted_piece(padded, row_start, col_start, height, width):
    zero_start = jnp.zeros((), jnp.int32)
    return lax.dynamic_slice(
        padded, (row_start, col_start, zero_start), (height, width, padded.shape[2])
    )


def block_forward(padded, resident, weight_slot, dilation, keep_rows):
    height, width, channels = resident.shape
    total = jnp.zeros((height * width, channels), jnp.float32)
    for row_step in (-1, 0, 1):
        for col_step in (-1, 0, 1):
            tap_index = 3 * (row_step + 1) + col_step + 1
            piece = shifted_piece(
                padded, HALO + row_step * dilation, HALO + col_step * dilation, height, width
            )
            total = total + jnp.dot(
                piece.reshape(height * width, channels),
                weight_slot[tap_index],
                preferred_element_type=jnp.float32,
            )
    summed = resident.astype(jnp.float32) + total.reshape(height, width, channels)
    return (summed * keep_rows[:, None, None]).astype(jnp.bfloat16)


def block_backward(padded_act, padded_cot, masked_cot, resident, weight_slot, dilation):
    height, width, channels = masked_cot.shape
    flat_cot = masked_cot.reshape(height * width, channels)
    weight_terms = []
    back_sum = jnp.zeros((height * width, channels), jnp.float32)
    for row_step in (-1, 0, 1):
        for col_step in (-1, 0, 1):
            tap_index = 3 * (row_step + 1) + col_step + 1
            act_piece = shifted_piece(
                padded_act, HALO + row_step * dilation, HALO + col_step * dilation, height, width
            )
            weight_terms.append(
                jnp.einsum(
                    "pc,pd->cd",
                    act_piece.reshape(height * width, channels),
                    flat_cot,
                    preferred_element_type=jnp.float32,
                )
            )
            cot_piece = shifted_piece(
                padded_cot, HALO - row_step * dilation, HALO - col_step * dilation, height, width
            )
            back_sum = back_sum + jnp.einsum(
                "pd,cd->pc",
                cot_piece.reshape(height * width, channels),
                weight_slot[tap_index],
                preferred_element_type=jnp.float32,
            )
    resident_f = resident.astype(jnp.float32).reshape(height * width, channels)
    slope = jnp.where(resident_f > 0, 1.0, jnp.exp(jnp.minimum(resident_f, 0.0)))
    new_cot = (flat_cot.astype(jnp.float32) + slope * back_sum).astype(jnp.bfloat16)
    return (jnp.stack(weight_terms), new_cot.reshape(height, width, channels))


def store_slot(saved, slot_index, micro_clip, values, running):
    current = saved[slot_index, micro_clip]
    return saved.at[slot_index, micro_clip].set(jnp.where(running, values, current))


def relay_body(features, residues, blocks, weights, cotangent):
    segment_count = lax.axis_size("segment")
    segment_index = lax.axis_index("segment")
    micro_count = features.shape[0]
    height, width, channels = (features.shape[1], features.shape[2], features.shape[3])
    slot_count = weights.shape[1]
    row_first = lax.axis_index("row") * height
    row_ids = row_first + jnp.arange(height, dtype=jnp.int32)
    active_blocks = blocks[0]
    weight_here = weights[0]
    dilations = [
        jnp.left_shift(jnp.int32(1), (slot_count * segment_index + slot_index) % 4)
        for slot_index in range(slot_count)
    ]
    tick_total = segment_count + micro_count - 1
    zero_value = jnp.zeros((), jnp.bfloat16)

    def forward_tick(tick_index, carry):
        incoming, saved_act, saved_res = carry
        micro = tick_index - segment_index
        running = (micro >= 0) & (micro < micro_count)
        micro_clip = jnp.clip(micro, 0, micro_count - 1)
        limit = residues[micro_clip]
        first_input = jnp.where((row_ids < limit)[:, None, None], features[micro_clip], zero_value)
        resident = jnp.where(segment_index == 0, first_input, incoming)
        keep_rows = (row_ids < limit).astype(jnp.float32)
        for slot_index in range(slot_count):
            active_here = running & (slot_index < active_blocks)
            activation = elu_rounded(resident)
            bordered = padded_2(activation, (("row", 0),), HALO)
            padded = widen_columns(bordered)
            saved_act = store_slot(saved_act, slot_index, micro_clip, padded, running)
            saved_res = store_slot(saved_res, slot_index, micro_clip, resident, running)
            resident = lax.cond(
                active_here,
                lambda packed: block_forward(
                    packed[0], packed[1], weight_here[slot_index], dilations[slot_index], keep_rows
                ),
                lambda packed: packed[1],
                (padded, resident),
            )
        outgoing = passed_along(resident, "segment", 1)
        return (outgoing, saved_act, saved_res)

    saved_act = jnp.zeros(
        (slot_count, micro_count, height + 2 * HALO, width + 2 * HALO, channels), jnp.bfloat16
    )
    saved_res = jnp.zeros((slot_count, micro_count, height, width, channels), jnp.bfloat16)
    start_carry = (jnp.zeros((height, width, channels), jnp.bfloat16), saved_act, saved_res)
    last_out, saved_act, saved_res = lax.fori_loop(0, tick_total, forward_tick, start_carry)

    def backward_tick(tick_index, carry):
        incoming, grads = carry
        micro = tick_index - (segment_count - 1 - segment_index)
        running = (micro >= 0) & (micro < micro_count)
        micro_clip = jnp.clip(micro, 0, micro_count - 1)
        keep_mask = (row_ids < residues[micro_clip])[:, None, None]
        grad_now = jnp.where(segment_index == segment_count - 1, cotangent[micro_clip], incoming)
        for slot_index in reversed(range(slot_count)):
            active_here = running & (slot_index < active_blocks)
            resident = saved_res[slot_index, micro_clip]
            masked_cot = jnp.where(keep_mask, grad_now, zero_value)
            padded_cot = widen_columns(padded_2(masked_cot, (("row", 0),), HALO))
            padded_act = saved_act[slot_index, micro_clip]
            weight_grad, grad_now = lax.cond(
                active_here,
                lambda packed: block_backward(
                    packed[0],
                    packed[1],
                    packed[2],
                    packed[3],
                    weight_here[slot_index],
                    dilations[slot_index],
                ),
                lambda packed: (jnp.zeros((9, channels, channels), jnp.float32), packed[4]),
                (padded_act, padded_cot, masked_cot, resident, grad_now),
            )
            grads = grads.at[slot_index].add(weight_grad)
        outgoing = passed_along(grad_now, "segment", -1)
        return (outgoing, grads)

    grad_start = (
        jnp.zeros((height, width, channels), jnp.bfloat16),
        jnp.zeros((slot_count, 9, channels, channels), jnp.float32),
    )
    last_cot, grads = lax.fori_loop(0, tick_total, backward_tick, grad_start)
    summed = lax.psum(grads.astype(jnp.bfloat16), ("row", "dp")).astype(jnp.float32)
    return summed[None]


VMEM_BUDGET = 44 * 2**20
CHUNK = 8


def chain_kernel(
    slots, parts, segments,
    info, blocks, features, cotangent, weights, weights_t, grads,
    saved, wide, grad_now, sums,
):
    rows, width, channels = features.shape
    rc = CHUNK
    cells = rc * width
    limit, own_segment, part = info[0], info[1], info[2]
    total = segments * slots
    own_rows = rows // parts
    column = lax.broadcasted_iota(jnp.int32, (rc, width, channels), 1).reshape(cells, channels)
    cell = lax.broadcasted_iota(jnp.int32, (cells, channels), 0)
    before = []
    count = jnp.int32(0)
    for section in range(segments):
        for slot in range(slots):
            before.append(count + jnp.minimum(slot, blocks[section]))
        count = count + blocks[section]

    def widened(values, dilation, first, sign):
        ahead = pltpu.roll(values, cells - dilation, 0)
        ahead = jnp.where(column < width - dilation, ahead, 0.0)
        behind = pltpu.roll(values, dilation, 0)
        behind = jnp.where(column >= dilation, behind, 0.0)
        left, right = (behind, ahead) if sign > 0 else (ahead, behind)
        at = pl.ds(HALO + first, rc)
        shape = (rc, width, channels)
        wide[at, :, 0:channels] = left.astype(jnp.bfloat16).reshape(shape)
        wide[at, :, channels:2 * channels] = values.astype(jnp.bfloat16).reshape(shape)
        wide[at, :, 2 * channels:] = right.astype(jnp.bfloat16).reshape(shape)

    def conv(taps, index, dilation, first, sign):
        out = None
        for row_step in (-1, 0, 1):
            piece = wide[pl.ds(HALO + first + sign * row_step * dilation, rc)]
            term = jnp.dot(
                piece.reshape(cells, 3 * channels),
                taps[index, row_step + 1],
                preferred_element_type=jnp.float32,
            )
            out = term if out is None else out + term
        return out

    wide[0:HALO] = jnp.zeros((HALO, width, 3 * channels), jnp.bfloat16)
    wide[HALO + rows:] = jnp.zeros((HALO, width, 3 * channels), jnp.bfloat16)
    grads[...] = jnp.zeros_like(grads)

    @pl.loop(0, rows // rc)
    def _(i):
        first = i * rc
        values = features[pl.ds(first, rc)].reshape(cells, channels).astype(jnp.float32)
        values = jnp.where(cell < (limit - first) * width, values, 0.0)
        saved[0, pl.ds(first, rc)] = values.astype(jnp.bfloat16).reshape(rc, width, channels)

    for index in range(total - 1):
        section, slot = divmod(index, slots)
        dilation = 2 ** (index % 4)
        source = before[index]

        @pl.when((slot < blocks[section]) & (source < count - 1))
        def _():
            @pl.loop(0, rows // rc)
            def _(i):
                first = i * rc
                x = saved[source, pl.ds(first, rc)].reshape(cells, channels).astype(jnp.float32)
                act = jnp.where(x > 0, x, jnp.exp(jnp.minimum(x, 0.0)) - 1.0)
                widened(act, dilation, first, 1)

            @pl.loop(0, rows // rc)
            def _(i):
                first = i * rc
                out = conv(weights, index, dilation, first, 1)
                x = saved[source, pl.ds(first, rc)].reshape(cells, channels).astype(jnp.float32)
                x = jnp.where(cell < (limit - first) * width, x + out, 0.0)
                saved[source + 1, pl.ds(first, rc)] = x.astype(jnp.bfloat16).reshape(rc, width, channels)

    grad_now[...] = cotangent[...]

    for index in reversed(range(total)):
        section, slot = divmod(index, slots)
        dilation = 2 ** (index % 4)
        source = before[index]
        active = (slot < blocks[section]) & (section >= own_segment)

        @pl.when(active)
        def _():
            @pl.loop(0, rows // rc)
            def _(i):
                first = i * rc
                g = grad_now[pl.ds(first, rc)].reshape(cells, channels).astype(jnp.float32)
                g = jnp.where(cell < (limit - first) * width, g, 0.0)
                widened(g, dilation, first, -1 * -1)

        @pl.when(active & (section == own_segment))
        def _():
            sums[...] = jnp.zeros_like(sums)

            @pl.loop(0, own_rows // rc)
            def _(i):
                first = part * own_rows + i * rc
                x = saved[source, pl.ds(first, rc)].reshape(cells, channels).astype(jnp.float32)
                act = jnp.where(x > 0, x, jnp.exp(jnp.minimum(x, 0.0)) - 1.0).astype(jnp.bfloat16)
                for row_step in (-1, 0, 1):
                    piece = wide[pl.ds(HALO + first - row_step * dilation, rc)]
                    sums[row_step + 1] += lax.dot_general(
                        act, piece.reshape(cells, 3 * channels),
                        (((0,), (0,)), ((), ())),
                        preferred_element_type=jnp.float32,
                    )

            for row_tap in range(3):
                for col_tap in range(3):
                    grads[slot, 3 * row_tap + col_tap] = sums[
                        row_tap, :, (2 - col_tap) * channels:(3 - col_tap) * channels
                    ].astype(jnp.bfloat16)

        @pl.when(active & ((section > own_segment) | (slot > 0)))
        def _():
            @pl.loop(0, rows // rc)
            def _(i):
                first = i * rc
                out = conv(weights_t, index, dilation, first, -1)
                x = saved[source, pl.ds(first, rc)].reshape(cells, channels).astype(jnp.float32)
                slope = jnp.where(x > 0, 1.0, jnp.exp(jnp.minimum(x, 0.0)))
                masked = wide[pl.ds(HALO + first, rc), :, channels:2 * channels]
                g = masked.reshape(cells, channels).astype(jnp.float32) + slope * out
                grad_now[pl.ds(first, rc)] = g.astype(jnp.bfloat16).reshape(rc, width, channels)


def whole_map_body(features, residues, blocks, weights, cotangent):
    micro_count, height, width, channels = features.shape
    slots = weights.shape[1]
    segments = lax.axis_size("segment")
    row_count = lax.axis_size("row")
    parts = row_count // micro_count
    rows = height * row_count
    row_index = lax.axis_index("row")
    micro = row_index // parts
    info = jnp.stack([residues[micro], lax.axis_index("segment"), row_index % parts])
    all_blocks = lax.all_gather(blocks, "segment", tiled=True)
    taps = lax.all_gather(weights, "segment", tiled=True)
    own = lax.all_gather(features, "row", axis=1, tiled=True)[micro]
    own_cot = lax.all_gather(cotangent, "row", axis=1, tiled=True)[micro]
    flat = taps.reshape(segments * slots, 3, 3, channels, channels)
    straight = flat.reshape(segments * slots, 3, 3 * channels, channels)
    turned = jnp.swapaxes(flat[:, :, ::-1], -1, -2).reshape(segments * slots, 3, 3 * channels, channels)
    smem = pl.BlockSpec(memory_space=pltpu.SMEM)
    vmem = pl.BlockSpec(memory_space=pltpu.VMEM)
    grads = pl.pallas_call(
        functools.partial(chain_kernel, slots, parts, segments),
        out_shape=jax.ShapeDtypeStruct((slots, 9, channels, channels), jnp.bfloat16),
        in_specs=[smem, smem, vmem, vmem, vmem, vmem],
        out_specs=vmem,
        scratch_shapes=[
            pltpu.VMEM((segments * slots, rows, width, channels), jnp.bfloat16),
            pltpu.VMEM((rows + 2 * HALO, width, 3 * channels), jnp.bfloat16),
            pltpu.VMEM((rows, width, channels), jnp.bfloat16),
            pltpu.VMEM((3, channels, 3 * channels), jnp.float32),
        ],
        compiler_params=pltpu.CompilerParams(vmem_limit_bytes=VMEM_BUDGET),
        name="chain",
    )(info, all_blocks, own, own_cot, straight, turned)
    return lax.psum(grads, ("row", "dp")).astype(jnp.float32)[None]


def body(features, residues, blocks, weights, cotangent):
    micro_count, height, width, channels = features.shape
    row_count, segments = lax.axis_size("row"), lax.axis_size("segment")
    one_map = height * row_count * width * channels * 2
    need = one_map * (weights.shape[1] * segments + 9) + 6 * segments * weights.size
    fits = need < VMEM_BUDGET and row_count % micro_count == 0
    fits = fits and (height * micro_count) % CHUNK == 0
    run = whole_map_body if fits else relay_body
    return run(features, residues, blocks, weights, cotangent)


def solution(mesh):
    in_specs = (
        P("dp", "row", None, None),
        P("dp"),
        P("segment"),
        P("segment", None, None, None, None),
        P("dp", "row", None, None),
    )
    out_specs = P("segment", None, None, None, None)
    return jax.shard_map(body, mesh=mesh, in_specs=in_specs, out_specs=out_specs, check_vma=False)
```

```python
import functools

import jax
import jax.numpy as jnp
from jax import lax
from jax.experimental import pallas as pl
from jax.experimental.pallas import tpu as pltpu
from jax.sharding import PartitionSpec as P

HALO = 8


def padded_2(block, sides, width):
    for axis, dim in sides:
        count = lax.axis_size(axis)
        forward = [(i, i + 1) for i in range(count - 1)]
        backward = [(target, source) for source, target in forward]
        low = lax.ppermute(
            lax.slice_in_dim(block, block.shape[dim] - width, None, axis=dim), axis, forward
        )
        high = lax.ppermute(lax.slice_in_dim(block, 0, width, axis=dim), axis, backward)
        block = jnp.concatenate([low, block, high], axis=dim)
    return block


def passed_along(value, axis, steps):
    count = lax.axis_size(axis)
    leading, last = (max(0, -steps), min(count, count - steps))
    return lax.ppermute(value, axis, [(source, source + steps) for source in range(leading, last)])


def widen_columns(values):
    return jnp.pad(values, ((0, 0), (HALO, HALO), (0, 0)))


def elu_rounded(values):
    return jax.nn.elu(values.astype(jnp.float32)).astype(jnp.bfloat16)


def shifted_piece(padded, row_start, col_start, height, width):
    zero_start = jnp.zeros((), jnp.int32)
    return lax.dynamic_slice(
        padded, (row_start, col_start, zero_start), (height, width, padded.shape[2])
    )


def block_forward(padded, resident, weight_slot, dilation, keep_rows):
    height, width, channels = resident.shape
    total = jnp.zeros((height * width, channels), jnp.float32)
    for row_step in (-1, 0, 1):
        for col_step in (-1, 0, 1):
            tap_index = 3 * (row_step + 1) + col_step + 1
            piece = shifted_piece(
                padded, HALO + row_step * dilation, HALO + col_step * dilation, height, width
            )
            total = total + jnp.dot(
                piece.reshape(height * width, channels),
                weight_slot[tap_index],
                preferred_element_type=jnp.float32,
            )
    summed = resident.astype(jnp.float32) + total.reshape(height, width, channels)
    return (summed * keep_rows[:, None, None]).astype(jnp.bfloat16)


def block_backward(padded_act, padded_cot, masked_cot, resident, weight_slot, dilation):
    height, width, channels = masked_cot.shape
    flat_cot = masked_cot.reshape(height * width, channels)
    weight_terms = []
    back_sum = jnp.zeros((height * width, channels), jnp.float32)
    for row_step in (-1, 0, 1):
        for col_step in (-1, 0, 1):
            tap_index = 3 * (row_step + 1) + col_step + 1
            act_piece = shifted_piece(
                padded_act, HALO + row_step * dilation, HALO + col_step * dilation, height, width
            )
            weight_terms.append(
                jnp.einsum(
                    "pc,pd->cd",
                    act_piece.reshape(height * width, channels),
                    flat_cot,
                    preferred_element_type=jnp.float32,
                )
            )
            cot_piece = shifted_piece(
                padded_cot, HALO - row_step * dilation, HALO - col_step * dilation, height, width
            )
            back_sum = back_sum + jnp.einsum(
                "pd,cd->pc",
                cot_piece.reshape(height * width, channels),
                weight_slot[tap_index],
                preferred_element_type=jnp.float32,
            )
    resident_f = resident.astype(jnp.float32).reshape(height * width, channels)
    slope = jnp.where(resident_f > 0, 1.0, jnp.exp(jnp.minimum(resident_f, 0.0)))
    new_cot = (flat_cot.astype(jnp.float32) + slope * back_sum).astype(jnp.bfloat16)
    return (jnp.stack(weight_terms), new_cot.reshape(height, width, channels))


def store_slot(saved, slot_index, micro_clip, values, running):
    current = saved[slot_index, micro_clip]
    return saved.at[slot_index, micro_clip].set(jnp.where(running, values, current))


def relay_body(features, residues, blocks, weights, cotangent):
    segment_count = lax.axis_size("segment")
    segment_index = lax.axis_index("segment")
    micro_count = features.shape[0]
    height, width, channels = (features.shape[1], features.shape[2], features.shape[3])
    slot_count = weights.shape[1]
    row_first = lax.axis_index("row") * height
    row_ids = row_first + jnp.arange(height, dtype=jnp.int32)
    active_blocks = blocks[0]
    weight_here = weights[0]
    dilations = [
        jnp.left_shift(jnp.int32(1), (slot_count * segment_index + slot_index) % 4)
        for slot_index in range(slot_count)
    ]
    tick_total = segment_count + micro_count - 1
    zero_value = jnp.zeros((), jnp.bfloat16)

    def forward_tick(tick_index, carry):
        incoming, saved_act, saved_res = carry
        micro = tick_index - segment_index
        running = (micro >= 0) & (micro < micro_count)
        micro_clip = jnp.clip(micro, 0, micro_count - 1)
        limit = residues[micro_clip]
        first_input = jnp.where((row_ids < limit)[:, None, None], features[micro_clip], zero_value)
        resident = jnp.where(segment_index == 0, first_input, incoming)
        keep_rows = (row_ids < limit).astype(jnp.float32)
        for slot_index in range(slot_count):
            active_here = running & (slot_index < active_blocks)
            activation = elu_rounded(resident)
            bordered = padded_2(activation, (("row", 0),), HALO)
            padded = widen_columns(bordered)
            saved_act = store_slot(saved_act, slot_index, micro_clip, padded, running)
            saved_res = store_slot(saved_res, slot_index, micro_clip, resident, running)
            resident = lax.cond(
                active_here,
                lambda packed: block_forward(
                    packed[0], packed[1], weight_here[slot_index], dilations[slot_index], keep_rows
                ),
                lambda packed: packed[1],
                (padded, resident),
            )
        outgoing = passed_along(resident, "segment", 1)
        return (outgoing, saved_act, saved_res)

    saved_act = jnp.zeros(
        (slot_count, micro_count, height + 2 * HALO, width + 2 * HALO, channels), jnp.bfloat16
    )
    saved_res = jnp.zeros((slot_count, micro_count, height, width, channels), jnp.bfloat16)
    start_carry = (jnp.zeros((height, width, channels), jnp.bfloat16), saved_act, saved_res)
    last_out, saved_act, saved_res = lax.fori_loop(0, tick_total, forward_tick, start_carry)

    def backward_tick(tick_index, carry):
        incoming, grads = carry
        micro = tick_index - (segment_count - 1 - segment_index)
        running = (micro >= 0) & (micro < micro_count)
        micro_clip = jnp.clip(micro, 0, micro_count - 1)
        keep_mask = (row_ids < residues[micro_clip])[:, None, None]
        grad_now = jnp.where(segment_index == segment_count - 1, cotangent[micro_clip], incoming)
        for slot_index in reversed(range(slot_count)):
            active_here = running & (slot_index < active_blocks)
            resident = saved_res[slot_index, micro_clip]
            masked_cot = jnp.where(keep_mask, grad_now, zero_value)
            padded_cot = widen_columns(padded_2(masked_cot, (("row", 0),), HALO))
            padded_act = saved_act[slot_index, micro_clip]
            weight_grad, grad_now = lax.cond(
                active_here,
                lambda packed: block_backward(
                    packed[0],
                    packed[1],
                    packed[2],
                    packed[3],
                    weight_here[slot_index],
                    dilations[slot_index],
                ),
                lambda packed: (jnp.zeros((9, channels, channels), jnp.float32), packed[4]),
                (padded_act, padded_cot, masked_cot, resident, grad_now),
            )
            grads = grads.at[slot_index].add(weight_grad)
        outgoing = passed_along(grad_now, "segment", -1)
        return (outgoing, grads)

    grad_start = (
        jnp.zeros((height, width, channels), jnp.bfloat16),
        jnp.zeros((slot_count, 9, channels, channels), jnp.float32),
    )
    last_cot, grads = lax.fori_loop(0, tick_total, backward_tick, grad_start)
    summed = lax.psum(grads.astype(jnp.bfloat16), ("row", "dp")).astype(jnp.float32)
    return summed[None]


VMEM_BUDGET = 44 * 2**20
CHUNK = 8


def chain_kernel(
    slots, parts, segments,
    info, blocks, features, cotangent, weights, weights_t, grads,
    saved, wide, grad_now, sums,
):
    rows, width, channels = features.shape
    rc = CHUNK
    cells = rc * width
    limit, own_segment, part = info[0], info[1], info[2]
    total = segments * slots
    own_rows = rows // parts
    column = lax.broadcasted_iota(jnp.int32, (rc, width, channels), 1).reshape(cells, channels)
    cell = lax.broadcasted_iota(jnp.int32, (cells, channels), 0)
    before = []
    count = jnp.int32(0)
    for section in range(segments):
        for slot in range(slots):
            before.append(count + jnp.minimum(slot, blocks[section]))
        count = count + blocks[section]

    def widened(values, dilation, first, sign):
        ahead = pltpu.roll(values, cells - dilation, 0)
        ahead = jnp.where(column < width - dilation, ahead, 0.0)
        behind = pltpu.roll(values, dilation, 0)
        behind = jnp.where(column >= dilation, behind, 0.0)
        left, right = (behind, ahead) if sign > 0 else (ahead, behind)
        at = pl.ds(HALO + first, rc)
        shape = (rc, width, channels)
        wide[at, :, 0:channels] = left.astype(jnp.bfloat16).reshape(shape)
        wide[at, :, channels:2 * channels] = values.astype(jnp.bfloat16).reshape(shape)
        wide[at, :, 2 * channels:] = right.astype(jnp.bfloat16).reshape(shape)

    def conv(taps, index, dilation, first, sign):
        out = None
        for row_step in (-1, 0, 1):
            piece = wide[pl.ds(HALO + first + sign * row_step * dilation, rc)]
            term = jnp.dot(
                piece.reshape(cells, 3 * channels),
                taps[index, row_step + 1],
                preferred_element_type=jnp.float32,
            )
            out = term if out is None else out + term
        return out

    wide[0:HALO] = jnp.zeros((HALO, width, 3 * channels), jnp.bfloat16)
    wide[HALO + rows:] = jnp.zeros((HALO, width, 3 * channels), jnp.bfloat16)
    grads[...] = jnp.zeros_like(grads)

    @pl.loop(0, rows // rc)
    def _(i):
        first = i * rc
        values = features[pl.ds(first, rc)].reshape(cells, channels).astype(jnp.float32)
        values = jnp.where(cell < (limit - first) * width, values, 0.0)
        saved[0, pl.ds(first, rc)] = values.astype(jnp.bfloat16).reshape(rc, width, channels)

    for index in range(total - 1):
        section, slot = divmod(index, slots)
        dilation = 2 ** (index % 4)
        source = before[index]

        @pl.when((slot < blocks[section]) & (source < count - 1))
        def _():
            @pl.loop(0, rows // rc)
            def _(i):
                first = i * rc
                x = saved[source, pl.ds(first, rc)].reshape(cells, channels).astype(jnp.float32)
                act = jnp.where(x > 0, x, jnp.exp(jnp.minimum(x, 0.0)) - 1.0)
                widened(act, dilation, first, 1)

            @pl.loop(0, rows // rc)
            def _(i):
                first = i * rc
                out = conv(weights, index, dilation, first, 1)
                x = saved[source, pl.ds(first, rc)].reshape(cells, channels).astype(jnp.float32)
                x = jnp.where(cell < (limit - first) * width, x + out, 0.0)
                saved[source + 1, pl.ds(first, rc)] = x.astype(jnp.bfloat16).reshape(rc, width, channels)

    grad_now[...] = cotangent[...]

    for index in reversed(range(total)):
        section, slot = divmod(index, slots)
        dilation = 2 ** (index % 4)
        source = before[index]
        active = (slot < blocks[section]) & (section >= own_segment)

        @pl.when(active)
        def _():
            @pl.loop(0, rows // rc)
            def _(i):
                first = i * rc
                g = grad_now[pl.ds(first, rc)].reshape(cells, channels).astype(jnp.float32)
                g = jnp.where(cell < (limit - first) * width, g, 0.0)
                widened(g, dilation, first, -1)

        @pl.when(active & (section == own_segment))
        def _():
            sums[...] = jnp.zeros_like(sums)

            @pl.loop(0, own_rows // rc)
            def _(i):
                first = part * own_rows + i * rc
                x = saved[source, pl.ds(first, rc)].reshape(cells, channels).astype(jnp.float32)
                act = jnp.where(x > 0, x, jnp.exp(jnp.minimum(x, 0.0)) - 1.0).astype(jnp.bfloat16)
                for row_step in (-1, 0, 1):
                    piece = wide[pl.ds(HALO + first - row_step * dilation, rc)]
                    sums[row_step + 1] += lax.dot_general(
                        act, piece.reshape(cells, 3 * channels),
                        (((0,), (0,)), ((), ())),
                        preferred_element_type=jnp.float32,
                    )

            for row_tap in range(3):
                for col_tap in range(3):
                    grads[slot, 3 * row_tap + col_tap] = sums[
                        row_tap, :, col_tap * channels:(col_tap + 1) * channels
                    ].astype(jnp.bfloat16)

        @pl.when(active & ((section > own_segment) | (slot > 0)))
        def _():
            @pl.loop(0, rows // rc)
            def _(i):
                first = i * rc
                out = conv(weights_t, index, dilation, first, -1)
                x = saved[source, pl.ds(first, rc)].reshape(cells, channels).astype(jnp.float32)
                slope = jnp.where(x > 0, 1.0, jnp.exp(jnp.minimum(x, 0.0)))
                masked = wide[pl.ds(HALO + first, rc), :, channels:2 * channels]
                g = masked.reshape(cells, channels).astype(jnp.float32) + slope * out
                grad_now[pl.ds(first, rc)] = g.astype(jnp.bfloat16).reshape(rc, width, channels)


def remote(source, target, send, recv, place):
    return pltpu.make_async_remote_copy(
        src_ref=source, dst_ref=target, send_sem=send, recv_sem=recv,
        device_id=place, device_id_type=pl.DeviceIdType.MESH,
    )


def greet(places):
    barrier = pltpu.get_barrier_semaphore()
    for place in places:
        pl.semaphore_signal(barrier, inc=1, device_id=place, device_id_type=pl.DeviceIdType.MESH)
    pl.semaphore_wait(barrier, len(places))


def gather_kernel(
    segments, row_count, pair, parts,
    features, cotangent, weights, counts,
    map_out, cot_out, taps_out, counts_out,
    map_send, map_recv, cot_send, cot_recv, tap_send, tap_recv, on_send, on_recv,
    count_send, count_recv, local,
):
    segment, row, core = lax.axis_index("segment"), lax.axis_index("row"), lax.axis_index("dp")
    height = features.shape[1]
    share = weights.shape[2] // pair
    mine = pl.ds(pl.multiple_of(core * share, share), share)
    band = pl.ds(row * height, height)
    row_peers = [lax.rem(row + k, row_count) for k in range(1, row_count)]
    segment_peers = [lax.rem(segment + k, segments) for k in range(1, segments)]
    core_peers = [lax.rem(core + k, pair) for k in range(1, pair)]
    greet(
        [{"row": peer} for peer in row_peers]
        + [{"segment": peer} for peer in segment_peers]
        + [{"dp": peer} for peer in core_peers]
    )
    taps, others = [], []
    for k, peer in enumerate(segment_peers):
        taps.append(remote(
            weights.at[0, :, mine], taps_out.at[segment, :, mine],
            tap_send.at[k], tap_recv.at[k], {"segment": peer},
        ))
        others.append(remote(
            counts, counts_out.at[segment], count_send.at[k], count_recv.at[k], {"segment": peer}
        ))
    for k, peer in enumerate(row_peers):
        others.append(remote(
            features.at[peer // parts], map_out.at[band], map_send.at[k], map_recv.at[k], {"row": peer}
        ))
        others.append(remote(
            cotangent.at[peer // parts], cot_out.at[band], cot_send.at[k], cot_recv.at[k], {"row": peer}
        ))
    for copy in taps + others:
        copy.start()
    kept = [
        pltpu.make_async_copy(features.at[row // parts], map_out.at[band], local.at[0]),
        pltpu.make_async_copy(cotangent.at[row // parts], cot_out.at[band], local.at[1]),
        pltpu.make_async_copy(weights.at[0], taps_out.at[segment], local.at[2]),
        pltpu.make_async_copy(counts, counts_out.at[segment], local.at[3]),
    ]
    for copy in kept:
        copy.start()
    passed = []
    for k in list(range(segments - 1)):
        taps[k].wait_recv()
        origin = lax.rem(segment - (k + 1) + segments, segments)
        for m, peer in enumerate(core_peers):
            copy = remote(
                taps_out.at[origin, :, mine], taps_out.at[origin, :, mine],
                on_send.at[k, m], on_recv.at[k, m], {"dp": peer},
            )
            copy.start()
            passed.append(copy)
    for copy in taps:
        copy.wait_send()
    for copy in others + passed + kept:
        copy.wait()


def reduce_kernel(row_count, pair, grads, out, slots, total, send, recv, send_back, recv_back):
    row, core = lax.axis_index("row"), lax.axis_index("dp")
    count = row_count * pair
    place = row * pair + core
    share = grads.shape[1] // count
    peers = [lax.rem(place + k, count) for k in range(1, count)]
    ids = [{"row": peer // pair, "dp": lax.rem(peer, pair)} for peer in peers]

    def piece(index):
        return pl.ds(pl.multiple_of(index * share, share), share)

    greet(ids)
    copies = [
        remote(grads.at[:, piece(peer)], slots.at[k], send.at[k], recv.at[k], ids[k])
        for k, peer in enumerate(peers)
    ]
    for copy in copies:
        copy.start()
    for copy in copies:
        copy.wait_recv()
    summed = grads[:, piece(place)].astype(jnp.float32)
    for k in range(count - 1):
        summed = summed + slots[k].astype(jnp.float32)
    total[...] = summed.astype(jnp.bfloat16)
    backs = [
        remote(total, out.at[:, piece(place)], send_back.at[k], recv_back.at[k], ids[k])
        for k in range(count - 1)
    ]
    for copy in backs:
        copy.start()
    out[:, piece(place)] = total[...]
    for copy in copies:
        copy.wait_send()
    for copy in backs:
        copy.wait()


def gathered(features, cotangent, weights, blocks, parts):
    micro_count, height, width, channels = features.shape
    segments, row_count, pair = [lax.axis_size(name) for name in ("segment", "row", "dp")]
    any_place = pl.BlockSpec(memory_space=pl.ANY)
    one_map = jax.ShapeDtypeStruct((height * row_count, width, channels), jnp.bfloat16)
    slot_taps = weights.shape[1] * weights.shape[2]
    dma = pltpu.SemaphoreType.DMA
    return pl.pallas_call(
        functools.partial(gather_kernel, segments, row_count, pair, parts),
        out_shape=[
            one_map, one_map,
            jax.ShapeDtypeStruct((segments, slot_taps, channels, channels), jnp.bfloat16),
            jax.ShapeDtypeStruct((segments, 8, 128), jnp.int32),
        ],
        in_specs=[any_place] * 4,
        out_specs=[any_place] * 4,
        scratch_shapes=[dma((row_count - 1,))] * 4 + [dma((segments - 1,))] * 2
        + [dma((segments - 1, pair - 1))] * 2 + [dma((segments - 1,))] * 2 + [dma((4,))],
        compiler_params=pltpu.CompilerParams(collective_id=0, has_side_effects=True),
        name="gather_all",
    )(
        features, cotangent, weights.reshape(1, slot_taps, channels, channels),
        jnp.broadcast_to(blocks[0], (8, 128)),
    )


def reduced(grads):
    row_count, pair = lax.axis_size("row"), lax.axis_size("dp")
    count = row_count * pair
    slot_taps, channels, _ = grads.shape
    piece = (slot_taps, channels // count, channels)
    vmem = pl.BlockSpec(memory_space=pltpu.VMEM)
    dma = pltpu.SemaphoreType.DMA
    return pl.pallas_call(
        functools.partial(reduce_kernel, row_count, pair),
        out_shape=jax.ShapeDtypeStruct(grads.shape, jnp.bfloat16),
        in_specs=[vmem],
        out_specs=vmem,
        scratch_shapes=[
            pltpu.VMEM((count - 1,) + piece, jnp.bfloat16),
            pltpu.VMEM(piece, jnp.bfloat16),
        ] + [dma((count - 1,))] * 4,
        compiler_params=pltpu.CompilerParams(
            collective_id=1, has_side_effects=True, vmem_limit_bytes=16 * 2**20
        ),
        name="reduce_all",
    )(grads)


def whole_map_body(features, residues, blocks, weights, cotangent):
    micro_count, height, width, channels = features.shape
    slots = weights.shape[1]
    segments = lax.axis_size("segment")
    row_count = lax.axis_size("row")
    parts = row_count // micro_count
    rows = height * row_count
    row_index = lax.axis_index("row")
    micro = row_index // parts
    info = jnp.stack([residues[micro], lax.axis_index("segment"), row_index % parts])
    own, own_cot, taps, counts = gathered(features, cotangent, weights, blocks, parts)
    all_blocks = counts[:, 0, 0]
    flat = taps.reshape(segments * slots, 3, 3, channels, channels)
    straight = flat.reshape(segments * slots, 3, 3 * channels, channels)
    turned = jnp.swapaxes(flat, -1, -2).reshape(segments * slots, 3, 3 * channels, channels)
    smem = pl.BlockSpec(memory_space=pltpu.SMEM)
    vmem = pl.BlockSpec(memory_space=pltpu.VMEM)
    grads = pl.pallas_call(
        functools.partial(chain_kernel, slots, parts, segments),
        out_shape=jax.ShapeDtypeStruct((slots, 9, channels, channels), jnp.bfloat16),
        in_specs=[smem, smem, vmem, vmem, vmem, vmem],
        out_specs=vmem,
        scratch_shapes=[
            pltpu.VMEM((segments * slots, rows, width, channels), jnp.bfloat16),
            pltpu.VMEM((rows + 2 * HALO, width, 3 * channels), jnp.bfloat16),
            pltpu.VMEM((rows, width, channels), jnp.bfloat16),
            pltpu.VMEM((3, channels, 3 * channels), jnp.float32),
        ],
        compiler_params=pltpu.CompilerParams(vmem_limit_bytes=VMEM_BUDGET),
        name="chain",
    )(info, all_blocks, own, own_cot, straight, turned)
    summed = reduced(grads.reshape(slots * 9, channels, channels))
    return summed.astype(jnp.float32).reshape(1, slots, 9, channels, channels)


def body(features, residues, blocks, weights, cotangent):
    micro_count, height, width, channels = features.shape
    row_count, segments = lax.axis_size("row"), lax.axis_size("segment")
    one_map = height * row_count * width * channels * 2
    need = one_map * (weights.shape[1] * segments + 9) + 6 * segments * weights.size
    fits = need < VMEM_BUDGET and row_count % micro_count == 0
    fits = fits and (height * micro_count) % CHUNK == 0
    fits = fits and channels % (16 * row_count * lax.axis_size("dp")) == 0
    run = whole_map_body if fits else relay_body
    return run(features, residues, blocks, weights, cotangent)


def solution(mesh):
    in_specs = (
        P("dp", "row", None, None),
        P("dp"),
        P("segment"),
        P("segment", None, None, None, None),
        P("dp", "row", None, None),
    )
    out_specs = P("segment", None, None, None, None)
    return jax.shard_map(body, mesh=mesh, in_specs=in_specs, out_specs=out_specs, check_vma=False)
```

```python
import functools

import jax
import jax.numpy as jnp
from jax import lax
from jax.experimental import pallas as pl
from jax.experimental.pallas import tpu as pltpu
from jax.sharding import PartitionSpec as P

HALO = 8


def padded_2(block, sides, width):
    for axis, dim in sides:
        count = lax.axis_size(axis)
        forward = [(i, i + 1) for i in range(count - 1)]
        backward = [(target, source) for source, target in forward]
        low = lax.ppermute(
            lax.slice_in_dim(block, block.shape[dim] - width, None, axis=dim), axis, forward
        )
        high = lax.ppermute(lax.slice_in_dim(block, 0, width, axis=dim), axis, backward)
        block = jnp.concatenate([low, block, high], axis=dim)
    return block


def passed_along(value, axis, steps):
    count = lax.axis_size(axis)
    leading, last = (max(0, -steps), min(count, count - steps))
    return lax.ppermute(value, axis, [(source, source + steps) for source in range(leading, last)])


def widen_columns(values):
    return jnp.pad(values, ((0, 0), (HALO, HALO), (0, 0)))


def elu_rounded(values):
    return jax.nn.elu(values.astype(jnp.float32)).astype(jnp.bfloat16)


def shifted_piece(padded, row_start, col_start, height, width):
    zero_start = jnp.zeros((), jnp.int32)
    return lax.dynamic_slice(
        padded, (row_start, col_start, zero_start), (height, width, padded.shape[2])
    )


def block_forward(padded, resident, weight_slot, dilation, keep_rows):
    height, width, channels = resident.shape
    total = jnp.zeros((height * width, channels), jnp.float32)
    for row_step in (-1, 0, 1):
        for col_step in (-1, 0, 1):
            tap_index = 3 * (row_step + 1) + col_step + 1
            piece = shifted_piece(
                padded, HALO + row_step * dilation, HALO + col_step * dilation, height, width
            )
            total = total + jnp.dot(
                piece.reshape(height * width, channels),
                weight_slot[tap_index],
                preferred_element_type=jnp.float32,
            )
    summed = resident.astype(jnp.float32) + total.reshape(height, width, channels)
    return (summed * keep_rows[:, None, None]).astype(jnp.bfloat16)


def block_backward(padded_act, padded_cot, masked_cot, resident, weight_slot, dilation):
    height, width, channels = masked_cot.shape
    flat_cot = masked_cot.reshape(height * width, channels)
    weight_terms = []
    back_sum = jnp.zeros((height * width, channels), jnp.float32)
    for row_step in (-1, 0, 1):
        for col_step in (-1, 0, 1):
            tap_index = 3 * (row_step + 1) + col_step + 1
            act_piece = shifted_piece(
                padded_act, HALO + row_step * dilation, HALO + col_step * dilation, height, width
            )
            weight_terms.append(
                jnp.einsum(
                    "pc,pd->cd",
                    act_piece.reshape(height * width, channels),
                    flat_cot,
                    preferred_element_type=jnp.float32,
                )
            )
            cot_piece = shifted_piece(
                padded_cot, HALO - row_step * dilation, HALO - col_step * dilation, height, width
            )
            back_sum = back_sum + jnp.einsum(
                "pd,cd->pc",
                cot_piece.reshape(height * width, channels),
                weight_slot[tap_index],
                preferred_element_type=jnp.float32,
            )
    resident_f = resident.astype(jnp.float32).reshape(height * width, channels)
    slope = jnp.where(resident_f > 0, 1.0, jnp.exp(jnp.minimum(resident_f, 0.0)))
    new_cot = (flat_cot.astype(jnp.float32) + slope * back_sum).astype(jnp.bfloat16)
    return (jnp.stack(weight_terms), new_cot.reshape(height, width, channels))


def store_slot(saved, slot_index, micro_clip, values, running):
    current = saved[slot_index, micro_clip]
    return saved.at[slot_index, micro_clip].set(jnp.where(running, values, current))


def relay_body(features, residues, blocks, weights, cotangent):
    segment_count = lax.axis_size("segment")
    segment_index = lax.axis_index("segment")
    micro_count = features.shape[0]
    height, width, channels = (features.shape[1], features.shape[2], features.shape[3])
    slot_count = weights.shape[1]
    row_first = lax.axis_index("row") * height
    row_ids = row_first + jnp.arange(height, dtype=jnp.int32)
    active_blocks = blocks[0]
    weight_here = weights[0]
    dilations = [
        jnp.left_shift(jnp.int32(1), (slot_count * segment_index + slot_index) % 4)
        for slot_index in range(slot_count)
    ]
    tick_total = segment_count + micro_count - 1
    zero_value = jnp.zeros((), jnp.bfloat16)

    def forward_tick(tick_index, carry):
        incoming, saved_act, saved_res = carry
        micro = tick_index - segment_index
        running = (micro >= 0) & (micro < micro_count)
        micro_clip = jnp.clip(micro, 0, micro_count - 1)
        limit = residues[micro_clip]
        first_input = jnp.where((row_ids < limit)[:, None, None], features[micro_clip], zero_value)
        resident = jnp.where(segment_index == 0, first_input, incoming)
        keep_rows = (row_ids < limit).astype(jnp.float32)
        for slot_index in range(slot_count):
            active_here = running & (slot_index < active_blocks)
            activation = elu_rounded(resident)
            bordered = padded_2(activation, (("row", 0),), HALO)
            padded = widen_columns(bordered)
            saved_act = store_slot(saved_act, slot_index, micro_clip, padded, running)
            saved_res = store_slot(saved_res, slot_index, micro_clip, resident, running)
            resident = lax.cond(
                active_here,
                lambda packed: block_forward(
                    packed[0], packed[1], weight_here[slot_index], dilations[slot_index], keep_rows
                ),
                lambda packed: packed[1],
                (padded, resident),
            )
        outgoing = passed_along(resident, "segment", 1)
        return (outgoing, saved_act, saved_res)

    saved_act = jnp.zeros(
        (slot_count, micro_count, height + 2 * HALO, width + 2 * HALO, channels), jnp.bfloat16
    )
    saved_res = jnp.zeros((slot_count, micro_count, height, width, channels), jnp.bfloat16)
    start_carry = (jnp.zeros((height, width, channels), jnp.bfloat16), saved_act, saved_res)
    last_out, saved_act, saved_res = lax.fori_loop(0, tick_total, forward_tick, start_carry)

    def backward_tick(tick_index, carry):
        incoming, grads = carry
        micro = tick_index - (segment_count - 1 - segment_index)
        running = (micro >= 0) & (micro < micro_count)
        micro_clip = jnp.clip(micro, 0, micro_count - 1)
        keep_mask = (row_ids < residues[micro_clip])[:, None, None]
        grad_now = jnp.where(segment_index == segment_count - 1, cotangent[micro_clip], incoming)
        for slot_index in reversed(range(slot_count)):
            active_here = running & (slot_index < active_blocks)
            resident = saved_res[slot_index, micro_clip]
            masked_cot = jnp.where(keep_mask, grad_now, zero_value)
            padded_cot = widen_columns(padded_2(masked_cot, (("row", 0),), HALO))
            padded_act = saved_act[slot_index, micro_clip]
            weight_grad, grad_now = lax.cond(
                active_here,
                lambda packed: block_backward(
                    packed[0],
                    packed[1],
                    packed[2],
                    packed[3],
                    weight_here[slot_index],
                    dilations[slot_index],
                ),
                lambda packed: (jnp.zeros((9, channels, channels), jnp.float32), packed[4]),
                (padded_act, padded_cot, masked_cot, resident, grad_now),
            )
            grads = grads.at[slot_index].add(weight_grad)
        outgoing = passed_along(grad_now, "segment", -1)
        return (outgoing, grads)

    grad_start = (
        jnp.zeros((height, width, channels), jnp.bfloat16),
        jnp.zeros((slot_count, 9, channels, channels), jnp.float32),
    )
    last_cot, grads = lax.fori_loop(0, tick_total, backward_tick, grad_start)
    summed = lax.psum(grads.astype(jnp.bfloat16), ("row", "dp")).astype(jnp.float32)
    return summed[None]


VMEM_BUDGET = 44 * 2**20
CHUNK = 8


def chain_kernel(
    slots, parts, segments,
    info, blocks, features, cotangent, taps_far, grads,
    saved, wide, grad_now, sums, taps, paired, loads,
):
    rows, width, channels = features.shape
    rc = CHUNK
    cells = rc * width
    limit, own_segment, part = info[0], info[1], info[2]
    total = segments * slots
    own_rows = rows // parts
    column = lax.broadcasted_iota(jnp.int32, (rc, width, channels), 1).reshape(cells, channels)
    cell = lax.broadcasted_iota(jnp.int32, (cells, channels), 0)
    fetches = [
        pltpu.make_async_copy(features, saved.at[0], loads.at[0]),
        pltpu.make_async_copy(taps_far, taps, loads.at[1]),
        pltpu.make_async_copy(cotangent, grad_now, loads.at[2]),
    ]
    for fetch in fetches:
        fetch.start()
    before, distance = [], []
    count, far, own_far = jnp.int32(0), jnp.int32(0), jnp.int32(0)
    for section in range(segments):
        own_far = jnp.where(section == own_segment, far, own_far)
        for slot in range(slots):
            before.append(count + jnp.minimum(slot, blocks[section]))
            distance.append(far)
            far = far + jnp.where(slot < blocks[section], 2 ** ((section * slots + slot) % 4), 0)
        count = count + blocks[section]

    def widened(values, dilation, first, sign):
        ahead = pltpu.roll(values, cells - dilation, 0)
        ahead = jnp.where(column < width - dilation, ahead, 0.0)
        behind = pltpu.roll(values, dilation, 0)
        behind = jnp.where(column >= dilation, behind, 0.0)
        left, right = (behind, ahead) if sign > 0 else (ahead, behind)
        at = pl.ds(HALO + first, rc)
        shape = (rc, width, channels)
        wide[at, :, 0:channels] = left.astype(jnp.bfloat16).reshape(shape)
        wide[at, :, channels:2 * channels] = values.astype(jnp.bfloat16).reshape(shape)
        wide[at, :, 2 * channels:] = right.astype(jnp.bfloat16).reshape(shape)

    def pair_up(tap_of):
        for row_tap in range(3):
            for col_tap in range(3):
                for column_block in range(2):
                    low = ((row_tap + column_block) * 3 + col_tap) * channels
                    paired[low:low + channels, column_block * channels:(column_block + 1) * channels] = (
                        tap_of(row_tap, col_tap)
                    )

    def conv(first, dilation):
        upper = [r for r in range(2 * rc) if (r // dilation) % 2 == 0]
        lines = [
            jnp.concatenate(
                [wide[HALO + first + r + (step - 1) * dilation] for r in upper], axis=0
            )
            for step in range(4)
        ]
        out = jnp.dot(
            jnp.concatenate(lines, axis=1), paired[...], preferred_element_type=jnp.float32
        )
        for place, r in enumerate(upper):
            piece = out[place * width:(place + 1) * width]
            yield first + r, piece[:, :channels]
            yield first + r + dilation, piece[:, channels:]

    wide[0:HALO] = jnp.zeros((HALO, width, 3 * channels), jnp.bfloat16)
    wide[HALO + rows:] = jnp.zeros((HALO, width, 3 * channels), jnp.bfloat16)
    grads[...] = jnp.zeros_like(grads)
    paired[...] = jnp.zeros_like(paired)
    fetches[0].wait()

    @pl.loop(0, rows // rc)
    def _(i):
        first = i * rc
        values = saved[0, pl.ds(first, rc)].reshape(cells, channels).astype(jnp.float32)
        values = jnp.where(cell < (limit - first) * width, values, 0.0)
        saved[0, pl.ds(first, rc)] = values.astype(jnp.bfloat16).reshape(rc, width, channels)

    fetches[1].wait()

    for index in range(total - 1):
        section, slot = divmod(index, slots)
        dilation = 2 ** (index % 4)
        source = before[index]

        @pl.when((slot < blocks[section]) & (source < count - 1))
        def _():
            @pl.loop(0, rows // rc)
            def _(i):
                first = i * rc
                x = saved[source, pl.ds(first, rc)].reshape(cells, channels).astype(jnp.float32)
                act = jnp.where(x > 0, x, jnp.exp(jnp.minimum(x, 0.0)) - 1.0)
                widened(act, dilation, first, 1)

            pair_up(lambda row_tap, col_tap: taps[section, slot * 9 + row_tap * 3 + col_tap])

            @pl.loop(0, rows // (2 * rc))
            def _(i):
                for r, out in conv(i * 2 * rc, dilation):
                    x = saved[source, r].astype(jnp.float32)
                    x = jnp.where(r < limit, x + out, 0.0)
                    saved[source + 1, r] = x.astype(jnp.bfloat16)

    fetches[2].wait()

    for index in reversed(range(total)):
        section, slot = divmod(index, slots)
        dilation = 2 ** (index % 4)
        source = before[index]
        active = (slot < blocks[section]) & (section >= own_segment)

        @pl.when(active)
        def _():
            @pl.loop(0, rows // rc)
            def _(i):
                first = i * rc
                g = grad_now[pl.ds(first, rc)].reshape(cells, channels).astype(jnp.float32)
                g = jnp.where(cell < (limit - first) * width, g, 0.0)
                widened(g, dilation, first, -1)

        @pl.when(active & (section == own_segment))
        def _():
            sums[...] = jnp.zeros_like(sums)

            @pl.loop(0, own_rows // rc)
            def _(i):
                first = part * own_rows + i * rc
                x = saved[source, pl.ds(first, rc)].reshape(cells, channels).astype(jnp.float32)
                act = jnp.where(x > 0, x, jnp.exp(jnp.minimum(x, 0.0)) - 1.0).astype(jnp.bfloat16)
                for row_step in (-1, 0, 1):
                    piece = wide[pl.ds(HALO + first - row_step * dilation, rc)]
                    sums[row_step + 1] += lax.dot_general(
                        act, piece.reshape(cells, 3 * channels),
                        (((0,), (0,)), ((), ())),
                        preferred_element_type=jnp.float32,
                    )

            for row_tap in range(3):
                for col_tap in range(3):
                    grads[slot, 3 * row_tap + col_tap] = sums[
                        row_tap, :, col_tap * channels:(col_tap + 1) * channels
                    ].astype(jnp.bfloat16)

        @pl.when(active & ((section > own_segment) | (slot > 0)))
        def _():
            pair_up(
                lambda row_tap, col_tap: taps[section, slot * 9 + (2 - row_tap) * 3 + col_tap].T
            )
            reach = distance[index] - own_far
            step = 2 * rc
            low = jnp.maximum(part * own_rows - reach, 0) // step
            high = (jnp.minimum((part + 1) * own_rows + reach, rows) + step - 1) // step

            @pl.loop(low, high)
            def _(i):
                for r, out in conv(i * step, dilation):
                    x = saved[source, r].astype(jnp.float32)
                    slope = jnp.where(x > 0, 1.0, jnp.exp(jnp.minimum(x, 0.0)))
                    masked = wide[HALO + r, :, channels:2 * channels].astype(jnp.float32)
                    grad_now[r] = (masked + slope * out).astype(jnp.bfloat16)


def remote(source, target, send, recv, place):
    return pltpu.make_async_remote_copy(
        src_ref=source, dst_ref=target, send_sem=send, recv_sem=recv,
        device_id=place, device_id_type=pl.DeviceIdType.MESH,
    )


def greet(places):
    barrier = pltpu.get_barrier_semaphore()
    for place in places:
        pl.semaphore_signal(barrier, inc=1, device_id=place, device_id_type=pl.DeviceIdType.MESH)
    pl.semaphore_wait(barrier, len(places))


def gather_kernel(
    segments, row_count, pair, parts,
    features, cotangent, weights, counts,
    map_out, cot_out, taps_out, counts_out,
    map_send, map_recv, cot_send, cot_recv, tap_send, tap_recv, on_send, on_recv,
    count_send, count_recv, local,
):
    segment, row, core = lax.axis_index("segment"), lax.axis_index("row"), lax.axis_index("dp")
    height = features.shape[1]
    share = weights.shape[2] // pair
    mine = pl.ds(pl.multiple_of(core * share, share), share)
    band = pl.ds(row * height, height)
    row_peers = [lax.rem(row + k, row_count) for k in range(1, row_count)]
    segment_peers = [lax.rem(segment + k, segments) for k in range(1, segments)]
    core_peers = [lax.rem(core + k, pair) for k in range(1, pair)]
    greet(
        [{"row": peer} for peer in row_peers]
        + [{"segment": peer} for peer in segment_peers]
        + [{"dp": peer} for peer in core_peers]
    )
    taps, others = [], []
    for k, peer in enumerate(segment_peers):
        taps.append(remote(
            weights.at[0, :, mine], taps_out.at[segment, :, mine],
            tap_send.at[k], tap_recv.at[k], {"segment": peer},
        ))
        others.append(remote(
            counts, counts_out.at[segment], count_send.at[k], count_recv.at[k], {"segment": peer}
        ))
    for k, peer in enumerate(row_peers):
        others.append(remote(
            features.at[peer // parts], map_out.at[band], map_send.at[k], map_recv.at[k], {"row": peer}
        ))
        others.append(remote(
            cotangent.at[peer // parts], cot_out.at[band], cot_send.at[k], cot_recv.at[k], {"row": peer}
        ))
    for copy in taps + others:
        copy.start()
    kept = [
        pltpu.make_async_copy(features.at[row // parts], map_out.at[band], local.at[0]),
        pltpu.make_async_copy(cotangent.at[row // parts], cot_out.at[band], local.at[1]),
        pltpu.make_async_copy(weights.at[0], taps_out.at[segment], local.at[2]),
        pltpu.make_async_copy(counts, counts_out.at[segment], local.at[3]),
    ]
    for copy in kept:
        copy.start()
    passed = []
    for k in list(range(segments - 1)):
        taps[k].wait_recv()
        origin = lax.rem(segment - (k + 1) + segments, segments)
        for m, peer in enumerate(core_peers):
            copy = remote(
                taps_out.at[origin, :, mine], taps_out.at[origin, :, mine],
                on_send.at[k, m], on_recv.at[k, m], {"dp": peer},
            )
            copy.start()
            passed.append(copy)
    for copy in taps:
        copy.wait_send()
    for copy in others + passed + kept:
        copy.wait()


def reduce_kernel(row_count, pair, grads, out, slots, total, send, recv, send_back, recv_back):
    row, core = lax.axis_index("row"), lax.axis_index("dp")
    count = row_count * pair
    place = row * pair + core
    share = grads.shape[1] // count
    peers = [lax.rem(place + k, count) for k in range(1, count)]
    ids = [{"row": peer // pair, "dp": lax.rem(peer, pair)} for peer in peers]

    def piece(index):
        return pl.ds(pl.multiple_of(index * share, share), share)

    greet(ids)
    copies = [
        remote(grads.at[:, piece(peer)], slots.at[k], send.at[k], recv.at[k], ids[k])
        for k, peer in enumerate(peers)
    ]
    for copy in copies:
        copy.start()
    for copy in copies:
        copy.wait_recv()
    summed = grads[:, piece(place)].astype(jnp.float32)
    for k in range(count - 1):
        summed = summed + slots[k].astype(jnp.float32)
    total[...] = summed.astype(jnp.bfloat16)
    backs = [
        remote(total, out.at[:, piece(place)], send_back.at[k], recv_back.at[k], ids[k])
        for k in range(count - 1)
    ]
    for copy in backs:
        copy.start()
    out[:, piece(place)] = total[...]
    for copy in copies:
        copy.wait_send()
    for copy in backs:
        copy.wait()


def gathered(features, cotangent, weights, blocks, parts):
    micro_count, height, width, channels = features.shape
    segments, row_count, pair = [lax.axis_size(name) for name in ("segment", "row", "dp")]
    any_place = pl.BlockSpec(memory_space=pl.ANY)
    one_map = jax.ShapeDtypeStruct((height * row_count, width, channels), jnp.bfloat16)
    slot_taps = weights.shape[1] * weights.shape[2]
    dma = pltpu.SemaphoreType.DMA
    return pl.pallas_call(
        functools.partial(gather_kernel, segments, row_count, pair, parts),
        out_shape=[
            one_map, one_map,
            jax.ShapeDtypeStruct((segments, slot_taps, channels, channels), jnp.bfloat16),
            jax.ShapeDtypeStruct((segments, 8, 128), jnp.int32),
        ],
        in_specs=[any_place] * 4,
        out_specs=[any_place] * 4,
        scratch_shapes=[dma((row_count - 1,))] * 4 + [dma((segments - 1,))] * 2
        + [dma((segments - 1, pair - 1))] * 2 + [dma((segments - 1,))] * 2 + [dma((4,))],
        compiler_params=pltpu.CompilerParams(collective_id=0, has_side_effects=True),
        name="gather_all",
    )(
        features, cotangent, weights.reshape(1, slot_taps, channels, channels),
        jnp.broadcast_to(blocks[0], (8, 128)),
    )


def reduced(grads):
    row_count, pair = lax.axis_size("row"), lax.axis_size("dp")
    count = row_count * pair
    slot_taps, channels, _ = grads.shape
    piece = (slot_taps, channels // count, channels)
    vmem = pl.BlockSpec(memory_space=pltpu.VMEM)
    dma = pltpu.SemaphoreType.DMA
    return pl.pallas_call(
        functools.partial(reduce_kernel, row_count, pair),
        out_shape=jax.ShapeDtypeStruct(grads.shape, jnp.bfloat16),
        in_specs=[vmem],
        out_specs=vmem,
        scratch_shapes=[
            pltpu.VMEM((count - 1,) + piece, jnp.bfloat16),
            pltpu.VMEM(piece, jnp.bfloat16),
        ] + [dma((count - 1,))] * 4,
        compiler_params=pltpu.CompilerParams(
            collective_id=1, has_side_effects=True, vmem_limit_bytes=16 * 2**20
        ),
        name="reduce_all",
    )(grads)


def whole_map_body(features, residues, blocks, weights, cotangent):
    micro_count, height, width, channels = features.shape
    slots = weights.shape[1]
    segments = lax.axis_size("segment")
    row_count = lax.axis_size("row")
    parts = row_count // micro_count
    rows = height * row_count
    row_index = lax.axis_index("row")
    micro = row_index // parts
    info = jnp.stack([residues[micro], lax.axis_index("segment"), row_index % parts])
    own, own_cot, taps, counts = gathered(features, cotangent, weights, blocks, parts)
    all_blocks = counts[:, 0, 0]
    smem = pl.BlockSpec(memory_space=pltpu.SMEM)
    vmem = pl.BlockSpec(memory_space=pltpu.VMEM)
    grads = pl.pallas_call(
        functools.partial(chain_kernel, slots, parts, segments),
        out_shape=jax.ShapeDtypeStruct((slots, 9, channels, channels), jnp.bfloat16),
        in_specs=[smem, smem] + [pl.BlockSpec(memory_space=pl.ANY)] * 3,
        out_specs=vmem,
        scratch_shapes=[
            pltpu.VMEM((segments * slots, rows, width, channels), jnp.bfloat16),
            pltpu.VMEM((rows + 2 * HALO, width, 3 * channels), jnp.bfloat16),
            pltpu.VMEM((rows, width, channels), jnp.bfloat16),
            pltpu.VMEM((3, channels, 3 * channels), jnp.float32),
            pltpu.VMEM((segments, slots * 9, channels, channels), jnp.bfloat16),
            pltpu.VMEM((12 * channels, 2 * channels), jnp.bfloat16),
            pltpu.SemaphoreType.DMA((3,)),
        ],
        compiler_params=pltpu.CompilerParams(vmem_limit_bytes=VMEM_BUDGET),
        name="chain",
    )(info, all_blocks, own, own_cot, taps)
    summed = reduced(grads.reshape(slots * 9, channels, channels))
    return summed.astype(jnp.float32).reshape(1, slots, 9, channels, channels)


def body(features, residues, blocks, weights, cotangent):
    micro_count, height, width, channels = features.shape
    row_count, segments = lax.axis_size("row"), lax.axis_size("segment")
    one_map = height * row_count * width * channels * 2
    need = one_map * (weights.shape[1] * segments + 9) + 6 * segments * weights.size
    fits = need < VMEM_BUDGET and row_count % micro_count == 0
    fits = fits and (height * micro_count) % CHUNK == 0
    fits = fits and (height * row_count) % (2 * CHUNK) == 0
    fits = fits and channels % (16 * row_count * lax.axis_size("dp")) == 0
    run = whole_map_body if fits else relay_body
    return run(features, residues, blocks, weights, cotangent)


def solution(mesh):
    in_specs = (
        P("dp", "row", None, None),
        P("dp"),
        P("segment"),
        P("segment", None, None, None, None),
        P("dp", "row", None, None),
    )
    out_specs = P("segment", None, None, None, None)
    return jax.shard_map(body, mesh=mesh, in_specs=in_specs, out_specs=out_specs, check_vma=False)
```
